32 devices in a mesh: groups: 2 (over x), pairs: 16 (over z, y, core), win: 1.
Axes of the slice: x: 2, y: 2, z: 4, core: 2. Of those that a mesh axis runs over, the one named last changes fastest.
Arguments:
- traces: bfloat16 [512, 3, 2, 2048], P(('groups', 'pairs'), None, 'win'), parts along dimension 0, may hold values from -6 to 6
- valid: int32 [512, 2], P(('groups', 'pairs'), 'win'), parts along dimension 0, may hold values 0 or 1
- pair_list: int32 [512, 2], P('groups'), parts along dimension 0, may hold values from 0 to 127, as said below
Outputs:
- stacks: float32 [512, 36, 2048], P(('groups', 'pairs', 'win')), parts along dimension 0
The draws below stay inside these ranges and needn't reach their ends.
There are 2 independent parts, one for each index of `groups`. The reference program is written for one: setup_inputs(seed, part) draws one part's arguments, and reference() takes and returns one part's arrays. A program takes and returns all parts, laid end to end along the dimension named above; each array names one. Nothing has to cross between parts.
Inputs may be any that keep to these rules, and one draw needn't show every extreme that they name: `pair_list`: row r belongs to owner r // 16, and block b to index b // 8 of pairs. The 32 entries of each owner name distinct blocks on exactly 8 indices of pairs, 4 on each.
All inputs are finite; a program needn't handle non-finite values. No bound on the sum of `valid` on one device may be relied on, other than what follows from the above.
Results may differ from the reference program's by a relative error of at most 0.0052.
Values may be sent and summed in bfloat16 or wider, within the bound.
A program may use at most 128 MiB of HBM per device.

```python
import math
import jax
import jax.numpy as jnp
from jax import lax

SAMPLES = 2048
BAND = 64
SB = 2
BLK_DEV = 8
PB = 16
CAP = 4
BLOCKS = 128
STATIONS = 256
WINDOWS = 2
PAIRBLOCKS = 256
CORRS = 36


def draw_pair_list(key, part):
    key = jax.random.fold_in(key, 7)
    owners = PAIRBLOCKS // PB
    groups_used = 2 * PB // CAP
    first_key, second_key, third_key = jax.random.split(key, 3)
    sources = jax.vmap(lambda single: jax.random.permutation(single, owners)[:groups_used])(jax.random.split(first_key, owners))

    def local_pick(single):
        return jax.vmap(lambda inner: jax.random.permutation(inner, BLK_DEV)[:CAP])(jax.random.split(single, groups_used))
    locals_drawn = jax.vmap(local_pick)(jax.random.split(second_key, owners))
    chosen = (sources[:, :, None] * BLK_DEV + locals_drawn).reshape(owners, 2 * PB)
    orders = jax.vmap(lambda single: jax.random.permutation(single, 2 * PB))(jax.random.split(third_key, owners))
    shuffled = jnp.take_along_axis(chosen, orders, axis=1)
    return shuffled.reshape(PAIRBLOCKS, 2).astype(jnp.int32)


def touch_ends(drawn, rng, low, largest):
    longest = drawn.shape.index(max(drawn.shape))
    spots = []
    for shift in (0, 1):
        where = [jax.random.randint(jax.random.fold_in(rng, axis), (), 0, length) for axis, length in enumerate(drawn.shape)]
        where[longest] = (where[longest] + shift) % drawn.shape[longest]
        spots.append(tuple(where))
    return drawn.at[spots[0]].set(low).at[spots[1]].set(largest)


def shard_levels(rng, extent, pieces, low, largest):
    factor_of, own = 1.0, jax.random.fold_in(rng, 6)
    for dim, shards_of in pieces:
        heights = jnp.exp(jax.random.uniform(jax.random.fold_in(own, dim), (shards_of,), jnp.float32, low / len(pieces), largest / len(pieces)))
        factor_of = factor_of * jnp.repeat(heights, extent[dim] // shards_of).reshape([-1 if axis == dim else 1 for axis in range(len(extent))])
    return factor_of


def centred(rng, extent, width, limit, cuts=(), kind=jnp.bfloat16):
    array = width * jax.random.normal(rng, extent, jnp.float32)
    if cuts:
        array = array * shard_levels(rng, extent, cuts, -0.22, 0.18)
    return jnp.clip(array, -limit, limit).astype(kind)


def setup_inputs(seed: int = 0, part: int = 0) -> dict:
    keys = jax.random.split(jax.random.key(seed), 4)
    part_splits = jax.random.split(jax.random.fold_in(keys[3], part), 4)
    traces = centred(part_splits[0], (STATIONS, 3, WINDOWS, SAMPLES), 1.0, 6.0, ((0, 16),))
    valid = touch_ends((jax.random.randint(part_splits[1], (STATIONS, WINDOWS), 0, 4) < 3).astype(jnp.int32), jax.random.fold_in(part_splits[1], 1), 0, 1)
    pair_list = draw_pair_list(jax.random.fold_in(jax.random.fold_in(keys[3], part), 71), part)
    return {"traces": traces, "valid": valid, "pair_list": pair_list}


def forward_table(samples):
    period = 2 * samples
    times = jnp.arange(samples, dtype=jnp.int32)[:, None]
    freqs = jnp.arange(samples, dtype=jnp.int32)[None, :]
    phase = (times * freqs % period).astype(jnp.float32) * (2.0 * math.pi / period)
    return jnp.concatenate([jnp.cos(phase), -jnp.sin(phase)], axis=1).astype(jnp.bfloat16)

def inverse_table(samples, first, count):
    period = 2 * samples
    freqs = (first + jnp.arange(count, dtype=jnp.int32))[:, None]
    lagged = jnp.arange(samples, dtype=jnp.int32)[None, :] - samples // 2
    phase = (freqs * lagged % period).astype(jnp.float32) * (2.0 * math.pi / period)
    weight = jnp.where(freqs == 0, 1.0, 2.0).astype(jnp.float32) / math.sqrt(2.0 * samples)
    return jnp.concatenate([weight * jnp.cos(phase), -weight * jnp.sin(phase)], axis=0).astype(jnp.bfloat16)

def transform(masked):
    samples = masked.shape[-1]
    spectrum = jnp.dot(masked.reshape(-1, samples), forward_table(samples), preferred_element_type=jnp.float32)
    spectrum = spectrum.reshape(masked.shape[:-1] + (2, samples))
    magnitude = jnp.sqrt(spectrum[..., 0, :] * spectrum[..., 0, :] + spectrum[..., 1, :] * spectrum[..., 1, :])
    band = magnitude.reshape(magnitude.shape[:-1] + (samples // BAND, BAND)).mean(axis=-1)
    spread = jnp.repeat(band, BAND, axis=-1)
    return (spectrum / (spread[..., None, :] + 1e-06)).astype(jnp.bfloat16)

def correlate(first, second):
    real_a = first[:, :, :, 0].astype(jnp.float32)[:, :, None]
    imag_a = first[:, :, :, 1].astype(jnp.float32)[:, :, None]
    real_b = second[:, :, :, 0].astype(jnp.float32)[:, None]
    imag_b = second[:, :, :, 1].astype(jnp.float32)[:, None]
    real_part = lax.optimization_barrier(jnp.sum(real_a * real_b + imag_a * imag_b, axis=3))
    imag_part = lax.optimization_barrier(jnp.sum(real_a * imag_b - imag_a * real_b, axis=3))
    joined = jnp.stack([real_part, imag_part], axis=3)
    rows = first.shape[1]
    return joined.reshape(first.shape[0], rows * rows, 2, first.shape[-1])

def reference(traces, valid, pair_list):
    masked = traces * valid[:, None, :, None].astype(traces.dtype)
    whitened = transform(masked)
    blocks = whitened.reshape(BLOCKS, SB * 3, WINDOWS, 2, SAMPLES)
    table = inverse_table(SAMPLES, 0, SAMPLES)

    def one_block(pair):
        first = jnp.take(blocks, pair[0:1], axis=0)
        second = jnp.take(blocks, pair[1:2], axis=0)
        cross = (correlate(first, second) / WINDOWS).astype(jnp.bfloat16)
        return jnp.dot(cross.reshape(CORRS, 2 * SAMPLES), table, preferred_element_type=jnp.float32)
    return lax.map(one_block, pair_list)
```

```python
import functools
import math

import jax
import jax.numpy as jnp
import ml_dtypes
import numpy as np
from jax import lax
from jax.experimental import pallas as pl
from jax.experimental.pallas import tpu as pltpu
from jax.sharding import PartitionSpec as P

BAND = 64
SB = 2
ROWS = SB * 3
CORRS = ROWS * ROWS
PAD = 40
TILE = 256


def tables(samples):
    period = 2 * samples
    angle = np.arange(period, dtype=np.float32) * np.float32(2.0 * math.pi / period)
    cosine, sine = np.cos(angle), np.sin(angle)
    index = np.arange(samples, dtype=np.int32)
    forward = index[:, None] * index[None, :] % period
    inverse = index[:, None] * (index[None, :] - samples // 2) % period
    weight = np.where(index[:, None] == 0, 1.0, 2.0).astype(np.float32) / np.float32(math.sqrt(period))
    first = np.stack([cosine[forward], -sine[forward]]).astype(ml_dtypes.bfloat16)
    second = np.stack([weight * cosine[inverse], -weight * sine[inverse]]).astype(ml_dtypes.bfloat16)
    return first, second


def stack_kernel(pairs, windows, x_ref, fwd_ref, band_ref, inv_ref, out_ref, white, cross, total):
    step = pl.program_id(0)
    steps = pl.num_programs(0)
    x = x_ref[...]
    real = jnp.dot(x, fwd_ref[0], preferred_element_type=jnp.float32)
    imag = jnp.dot(x, fwd_ref[1], preferred_element_type=jnp.float32)
    magnitude = jnp.sqrt(real * real + imag * imag)
    high = magnitude.astype(jnp.bfloat16)
    low = (magnitude - high.astype(jnp.float32)).astype(jnp.bfloat16)
    band = jnp.dot(high, band_ref[...], preferred_element_type=jnp.float32) + jnp.dot(
        low, band_ref[...], preferred_element_type=jnp.float32
    )
    scale = 1.0 / (band + 1e-06)
    white[0] = (real * scale).astype(jnp.bfloat16).astype(jnp.float32)
    white[1] = (imag * scale).astype(jnp.bfloat16).astype(jnp.float32)
    for lane in range(0, TILE, 128):
        lanes = slice(lane, lane + 128)
        for p0 in range(0, pairs, 8):

            def value(side, i, w, part):
                row = ((side * ROWS + i) * windows + w) * pairs + p0
                return white[part, row : row + 8, lanes]

            for i in range(ROWS):
                mine = [(value(0, i, w, 0), value(0, i, w, 1)) for w in range(windows)]
                for j in range(ROWS):
                    re = im = None
                    for w in range(windows):
                        ar, ai = mine[w]
                        br, bi = value(1, j, w, 0), value(1, j, w, 1)
                        re_w = ar * br + ai * bi
                        im_w = ar * bi - ai * br
                        re = re_w if re is None else re + re_w
                        im = im_w if im is None else im + im_w
                    spot = pl.ds(p0 * PAD + i * ROWS + j, 8, stride=PAD)
                    k = lane // 128
                    cross[0, k, spot, :] = re * (1.0 / windows)
                    cross[1, k, spot, :] = im * (1.0 / windows)
    count = TILE // 128
    both = jnp.concatenate(
        [cross[part, k].astype(jnp.bfloat16) for part in range(2) for k in range(count)], axis=1
    )
    samples = out_ref.shape[-1]
    wide = 512

    def lags(at):
        table = jnp.concatenate([inv_ref[0, :, at], inv_ref[1, :, at]], axis=0)
        return jnp.dot(both, table, preferred_element_type=jnp.float32)

    @pl.when(step == 0)
    def _():
        for t in range(0, samples, wide):
            total[:, t : t + wide] = lags(slice(t, t + wide))

    @pl.when((step > 0) & (step < steps - 1))
    def _():
        for t in range(0, samples, wide):
            total[:, t : t + wide] += lags(slice(t, t + wide))

    @pl.when(step == steps - 1)
    def _():
        for t in range(0, samples, wide):
            done = total[:, t : t + wide] + lags(slice(t, t + wide))
            for p in range(pairs):
                out_ref[p, :, t : t + wide] = done[p * PAD : p * PAD + CORRS]


def stack(x, pairs, windows):
    samples = x.shape[-1]
    first, second = tables(samples)
    runs = np.arange(TILE) // BAND
    band = ((runs[:, None] == runs[None, :]) / BAND).astype(ml_dtypes.bfloat16)
    return pl.pallas_call(
        functools.partial(stack_kernel, pairs, windows),
        out_shape=jax.ShapeDtypeStruct((pairs, CORRS, samples), jnp.float32),
        grid=(samples // TILE,),
        in_specs=[
            pl.BlockSpec(x.shape, lambda j: (0, 0)),
            pl.BlockSpec((2, samples, TILE), lambda j: (0, 0, j)),
            pl.BlockSpec((TILE, TILE), lambda j: (0, 0)),
            pl.BlockSpec((2, TILE, samples), lambda j: (0, j, 0)),
        ],
        out_specs=pl.BlockSpec((pairs, CORRS, samples), lambda j: (0, 0, 0)),
        scratch_shapes=[
            pltpu.VMEM((2, x.shape[0], TILE), jnp.float32),
            pltpu.VMEM((2, TILE // 128, pairs * PAD, 128), jnp.float32),
            pltpu.VMEM((pairs * PAD, samples), jnp.float32),
        ],
        compiler_params=pltpu.CompilerParams(vmem_limit_bytes=56 * 2**20),
        cost_estimate=pl.CostEstimate(
            flops=4 * (x.shape[0] + pairs * PAD) * samples * samples,
            bytes_accessed=8 * samples * samples + 4 * pairs * CORRS * samples,
            transcendentals=x.shape[0] * samples,
        ),
        name="stack",
    )(x, jnp.asarray(first), jnp.asarray(band), jnp.asarray(second))


def local(traces, valid, pair_list):
    owners = lax.axis_size("pairs")
    window_devs = lax.axis_size("win")
    samples = traces.shape[-1]
    per_window = traces.shape[2]
    windows = per_window * window_devs
    blk_count = traces.shape[0] // SB
    pairs = pair_list.shape[0] // (owners * window_devs)
    own_rows = blk_count * ROWS * per_window
    masked = traces * valid[:, None, :, None].astype(traces.dtype)
    everything = lax.all_gather(
        masked.reshape(own_rows, samples), ("pairs", "win"), axis=0, tiled=True
    )
    place = lax.axis_index("pairs") * window_devs + lax.axis_index("win")
    mine = lax.dynamic_slice_in_dim(pair_list, place * pairs, pairs, 0).T
    blocks = mine[:, None, None, None, :]
    i = jnp.arange(ROWS)[None, :, None, None, None]
    v = jnp.arange(window_devs)[None, None, :, None, None]
    w = jnp.arange(per_window)[None, None, None, :, None]
    device = blocks // blk_count * window_devs + v
    wanted = device * own_rows + ((blocks % blk_count) * ROWS + i) * per_window + w
    chosen = wanted.reshape(-1, 1) == jnp.arange(everything.shape[0])[None, :]
    x = jnp.dot(chosen.astype(jnp.bfloat16), everything, preferred_element_type=jnp.bfloat16)
    return stack(x, pairs, windows)


def solution(mesh):
    in_specs = (
        P(("groups", "pairs"), None, "win", None),
        P(("groups", "pairs"), "win"),
        P("groups", None),
    )
    out_specs = P(("groups", "pairs", "win"), None, None)
    return jax.shard_map(local, mesh=mesh, in_specs=in_specs, out_specs=out_specs, check_vma=False)
```

```python
import functools
import math

import jax
import jax.numpy as jnp
import ml_dtypes
import numpy as np
from jax import lax
from jax.experimental import pallas as pl
from jax.experimental.pallas import tpu as pltpu
from jax.sharding import PartitionSpec as P

BAND = 64
SB = 2
ROWS = SB * 3
CORRS = ROWS * ROWS
TILE = 256


def tables(samples):
    period = 2 * samples
    angle = np.arange(period, dtype=np.float32) * np.float32(2.0 * math.pi / period)
    cosine, sine = np.cos(angle), np.sin(angle)
    index = np.arange(samples, dtype=np.int32)
    forward = index[:, None] * index[None, :] % period
    inverse = index[:, None] * (index[None, :] - samples // 2) % period
    weight = np.where(index[:, None] == 0, 1.0, 2.0).astype(np.float32) / np.float32(math.sqrt(period))
    first = np.stack([cosine[forward], -sine[forward]]).astype(ml_dtypes.bfloat16)
    second = np.stack([weight * cosine[inverse], -weight * sine[inverse]]).astype(ml_dtypes.bfloat16)
    return first, second


def stack_kernel(pairs, windows, x_ref, fwd_ref, band_ref, inv_ref, out_ref, white, cross):
    @pl.when(pl.program_id(0) == 0)
    def _():
        out_ref[...] = jnp.zeros_like(out_ref)

    x = x_ref[...]
    real = jnp.dot(x, fwd_ref[0], preferred_element_type=jnp.float32)
    imag = jnp.dot(x, fwd_ref[1], preferred_element_type=jnp.float32)
    magnitude = jnp.sqrt(real * real + imag * imag)
    high = magnitude.astype(jnp.bfloat16)
    low = (magnitude - high.astype(jnp.float32)).astype(jnp.bfloat16)
    band = jnp.dot(high, band_ref[...], preferred_element_type=jnp.float32) + jnp.dot(
        low, band_ref[...], preferred_element_type=jnp.float32
    )
    scale = 1.0 / (band + 1e-06)
    white[0] = (real * scale).astype(jnp.bfloat16).astype(jnp.float32)
    white[1] = (imag * scale).astype(jnp.bfloat16).astype(jnp.float32)
    for lane in range(0, TILE, 128):
        lanes = slice(lane, lane + 128)
        for p0 in range(0, pairs, 8):

            def value(side, i, w, part):
                row = ((side * ROWS + i) * windows + w) * pairs + p0
                return white[part, row : row + 8, lanes]

            for i in range(ROWS):
                mine = [(value(0, i, w, 0), value(0, i, w, 1)) for w in range(windows)]
                for j in range(ROWS):
                    re = im = None
                    for w in range(windows):
                        ar, ai = mine[w]
                        br, bi = value(1, j, w, 0), value(1, j, w, 1)
                        re_w = ar * br + ai * bi
                        im_w = ar * bi - ai * br
                        re = re_w if re is None else re + re_w
                        im = im_w if im is None else im + im_w
                    row = (i * ROWS + j) * pairs + p0
                    cross[row : row + 8, lanes] = re * (1.0 / windows)
                    cross[row : row + 8, TILE + lane : TILE + lane + 128] = im * (1.0 / windows)
    both = cross[...].astype(jnp.bfloat16)
    samples = out_ref.shape[-1]
    wide = 512
    for t in range(0, samples, wide):
        table = jnp.concatenate([inv_ref[0, :, t : t + wide], inv_ref[1, :, t : t + wide]], axis=0)
        out_ref[:, t : t + wide] += jnp.dot(both, table, preferred_element_type=jnp.float32)


def stack(x, pairs, windows):
    samples = x.shape[-1]
    first, second = tables(samples)
    runs = np.arange(TILE) // BAND
    band = ((runs[:, None] == runs[None, :]) / BAND).astype(ml_dtypes.bfloat16)
    out = pl.pallas_call(
        functools.partial(stack_kernel, pairs, windows),
        out_shape=jax.ShapeDtypeStruct((CORRS * pairs, samples), jnp.float32),
        grid=(samples // TILE,),
        in_specs=[
            pl.BlockSpec(x.shape, lambda j: (0, 0)),
            pl.BlockSpec((2, samples, TILE), lambda j: (0, 0, j)),
            pl.BlockSpec((TILE, TILE), lambda j: (0, 0)),
            pl.BlockSpec((2, TILE, samples), lambda j: (0, j, 0)),
        ],
        out_specs=pl.BlockSpec((CORRS * pairs, samples), lambda j: (0, 0)),
        scratch_shapes=[
            pltpu.VMEM((2, x.shape[0], TILE), jnp.float32),
            pltpu.VMEM((CORRS * pairs, 2 * TILE), jnp.float32),
        ],
        compiler_params=pltpu.CompilerParams(vmem_limit_bytes=56 * 2**20),
        cost_estimate=pl.CostEstimate(
            flops=4 * (x.shape[0] + pairs * CORRS) * samples * samples,
            bytes_accessed=8 * samples * samples + 4 * pairs * CORRS * samples,
            transcendentals=x.shape[0] * samples,
        ),
        name="stack",
    )(x, jnp.asarray(first), jnp.asarray(band), jnp.asarray(second))
    return out.reshape(CORRS, pairs, samples).transpose(1, 0, 2)


def local(traces, valid, pair_list):
    owners = lax.axis_size("pairs")
    window_devs = lax.axis_size("win")
    me = lax.axis_index("pairs")
    samples = traces.shape[-1]
    per_window = traces.shape[2]
    windows = per_window * window_devs
    blk_count = traces.shape[0] // SB
    pair_count = pair_list.shape[0] // owners
    pairs = pair_count // window_devs
    capacity = max(1, 4 * pair_count // owners)
    series = ROWS * per_window
    masked = (traces * valid[:, None, :, None].astype(traces.dtype)).reshape(-1, samples)

    requests = pair_list.reshape(owners, 2 * pair_count)
    sources = requests // blk_count
    ids = jnp.arange(2 * pair_count, dtype=jnp.int32)
    earlier = ids[None, :] < ids[:, None]
    ranks = jnp.sum((sources[:, :, None] == sources[:, None, :]) & earlier[None], axis=-1)
    slots = jnp.arange(capacity, dtype=jnp.int32)
    found = (sources == me)[:, None, :] & (ranks[:, None, :] == slots[None, :, None])
    picked = jnp.sum(jnp.where(found, requests[:, None, :] % blk_count + 1, 0), axis=-1) - 1
    picked = jnp.broadcast_to(picked[:, None], (owners, window_devs, capacity)).reshape(-1, 1)
    serial = jnp.arange(series, dtype=jnp.int32)
    from_rows = jnp.where(picked < 0, -1, picked * series + serial).reshape(-1, 1)
    sending = from_rows == jnp.arange(masked.shape[0], dtype=jnp.int32)[None, :]
    sent = jnp.dot(sending.astype(jnp.bfloat16), masked, preferred_element_type=jnp.bfloat16)
    received = lax.all_to_all(
        sent.reshape(owners * window_devs, capacity * series, samples),
        ("pairs", "win"),
        split_axis=0,
        concat_axis=0,
        tiled=True,
    ).reshape(-1, samples)

    def kept(array):
        own = lax.dynamic_index_in_dim(array, me, 0, keepdims=False).reshape(pair_count, 2)
        own = lax.dynamic_slice_in_dim(own, lax.axis_index("win") * pairs, pairs, 0)
        return own.T[:, None, None, None, :]

    i = jnp.arange(ROWS, dtype=jnp.int32)[None, :, None, None, None]
    v = jnp.arange(window_devs, dtype=jnp.int32)[None, None, :, None, None]
    w = jnp.arange(per_window, dtype=jnp.int32)[None, None, None, :, None]
    slot = (kept(sources) * window_devs + v) * capacity + kept(ranks)
    wanted = (slot * ROWS + i) * per_window + w
    chosen = wanted.reshape(-1, 1) == jnp.arange(received.shape[0], dtype=jnp.int32)[None, :]
    x = jnp.dot(chosen.astype(jnp.bfloat16), received, preferred_element_type=jnp.bfloat16)
    return stack(x, pairs, windows)


def solution(mesh):
    in_specs = (
        P(("groups", "pairs"), None, "win", None),
        P(("groups", "pairs"), "win"),
        P("groups", None),
    )
    out_specs = P(("groups", "pairs", "win"), None, None)
    return jax.shard_map(local, mesh=mesh, in_specs=in_specs, out_specs=out_specs, check_vma=False)
```

```python
import functools
import math

import jax
import jax.numpy as jnp
import ml_dtypes
import numpy as np
from jax import lax
from jax.experimental import pallas as pl
from jax.experimental.pallas import tpu as pltpu
from jax.sharding import PartitionSpec as P

BAND = 64
SB = 2
ROWS = SB * 3
CORRS = ROWS * ROWS
TILE = 256


def tables(samples):
    period = 2 * samples
    angle = np.arange(period, dtype=np.float32) * np.float32(2.0 * math.pi / period)
    cosine, sine = np.cos(angle), np.sin(angle)
    index = np.arange(samples, dtype=np.int32)
    forward = index[:, None] * index[None, :] % period
    inverse = index[:, None] * (index[None, :] - samples // 2) % period
    weight = np.where(index[:, None] == 0, 1.0, 2.0).astype(np.float32) / np.float32(math.sqrt(period))
    first = np.stack([cosine[forward], -sine[forward]]).astype(ml_dtypes.bfloat16)
    second = np.stack([weight * cosine[inverse], -weight * sine[inverse]]).astype(ml_dtypes.bfloat16)
    return first, second


def stack_kernel(pairs, windows, x_ref, fwd_ref, band_ref, inv_ref, out_ref, white, cross):
    @pl.when(pl.program_id(0) == 0)
    def _():
        out_ref[...] = jnp.zeros_like(out_ref)

    x = x_ref[...]
    real = jnp.dot(x, fwd_ref[0], preferred_element_type=jnp.float32)
    imag = jnp.dot(x, fwd_ref[1], preferred_element_type=jnp.float32)
    magnitude = jnp.sqrt(real * real + imag * imag)
    high = magnitude.astype(jnp.bfloat16)
    low = (magnitude - high.astype(jnp.float32)).astype(jnp.bfloat16)
    band = jnp.dot(high, band_ref[...], preferred_element_type=jnp.float32) + jnp.dot(
        low, band_ref[...], preferred_element_type=jnp.float32
    )
    scale = 1.0 / (band + 1e-06)
    white[0] = (real * scale).astype(jnp.bfloat16).astype(jnp.float32)
    white[1] = (imag * scale).astype(jnp.bfloat16).astype(jnp.float32)
    for lane in range(0, TILE, 128):
        lanes = slice(lane, lane + 128)
        for p0 in range(0, pairs, 8):

            def value(side, i, w, part):
                row = ((side * ROWS + i) * windows + w) * pairs + p0
                return white[part, row : row + 8, lanes]

            for i in range(ROWS):
                mine = [(value(0, i, w, 0), value(0, i, w, 1)) for w in range(windows)]
                for j in range(ROWS):
                    re = im = None
                    for w in range(windows):
                        ar, ai = mine[w]
                        br, bi = value(1, j, w, 0), value(1, j, w, 1)
                        re_w = ar * br + ai * bi
                        im_w = ar * bi - ai * br
                        re = re_w if re is None else re + re_w
                        im = im_w if im is None else im + im_w
                    row = (i * ROWS + j) * pairs + p0
                    cross[row : row + 8, lanes] = re * (1.0 / windows)
                    cross[row : row + 8, TILE + lane : TILE + lane + 128] = im * (1.0 / windows)
    both = cross[...].astype(jnp.bfloat16)
    samples = out_ref.shape[-1]
    wide = 512
    for t in range(0, samples, wide):
        table = jnp.concatenate([inv_ref[0, :, t : t + wide], inv_ref[1, :, t : t + wide]], axis=0)
        out_ref[:, t : t + wide] += jnp.dot(both, table, preferred_element_type=jnp.float32)


def stack(x, pairs, windows):
    samples = x.shape[-1]
    first, second = tables(samples)
    runs = np.arange(TILE) // BAND
    band = ((runs[:, None] == runs[None, :]) / BAND).astype(ml_dtypes.bfloat16)
    out = pl.pallas_call(
        functools.partial(stack_kernel, pairs, windows),
        out_shape=jax.ShapeDtypeStruct((CORRS * pairs, samples), jnp.float32),
        grid=(samples // TILE,),
        in_specs=[
            pl.BlockSpec(x.shape, lambda j: (0, 0)),
            pl.BlockSpec((2, samples, TILE), lambda j: (0, 0, j)),
            pl.BlockSpec((TILE, TILE), lambda j: (0, 0)),
            pl.BlockSpec((2, TILE, samples), lambda j: (0, j, 0)),
        ],
        out_specs=pl.BlockSpec((CORRS * pairs, samples), lambda j: (0, 0)),
        scratch_shapes=[
            pltpu.VMEM((2, x.shape[0], TILE), jnp.float32),
            pltpu.VMEM((CORRS * pairs, 2 * TILE), jnp.float32),
        ],
        compiler_params=pltpu.CompilerParams(vmem_limit_bytes=56 * 2**20),
        cost_estimate=pl.CostEstimate(
            flops=4 * (x.shape[0] + pairs * CORRS) * samples * samples,
            bytes_accessed=8 * samples * samples + 4 * pairs * CORRS * samples,
            transcendentals=x.shape[0] * samples,
        ),
        name="stack",
    )(x, jnp.asarray(first), jnp.asarray(band), jnp.asarray(second))
    return out.reshape(CORRS, pairs, samples).transpose(1, 0, 2)


def exchange_kernel(count, window_devs, sent_ref, got_ref, send_sem, recv_sem, own_sem):
    me = lax.axis_index("pairs") * window_devs + lax.axis_index("win")
    group = lax.axis_index("groups")

    def device(index):
        return (group, index // window_devs, index % window_devs)

    def copy(distance):
        peer = lax.rem(me + distance, count)
        return pltpu.make_async_remote_copy(
            src_ref=sent_ref.at[peer],
            dst_ref=got_ref.at[me],
            send_sem=send_sem.at[distance],
            recv_sem=recv_sem.at[distance],
            device_id=device(peer),
            device_id_type=pl.DeviceIdType.MESH,
        )

    barrier = pltpu.get_barrier_semaphore()

    @pl.loop(1, count)
    def _(distance):
        pl.semaphore_signal(
            barrier,
            inc=1,
            device_id=device(lax.rem(me + distance, count)),
            device_id_type=pl.DeviceIdType.MESH,
        )

    pl.semaphore_wait(barrier, count - 1)

    @pl.loop(1, count)
    def _(distance):
        copy(distance).start()

    own = pltpu.make_async_copy(sent_ref.at[me], got_ref.at[me], own_sem)
    own.start()
    own.wait()

    @pl.loop(1, count)
    def _(distance):
        copy(distance).wait()


def exchange(sent, window_devs):
    count = sent.shape[0]
    return pl.pallas_call(
        functools.partial(exchange_kernel, count, window_devs),
        out_shape=jax.ShapeDtypeStruct(sent.shape, sent.dtype),
        in_specs=[pl.BlockSpec(memory_space=pltpu.VMEM)],
        out_specs=pl.BlockSpec(memory_space=pltpu.VMEM),
        scratch_shapes=[
            pltpu.SemaphoreType.DMA((count,)),
            pltpu.SemaphoreType.DMA((count,)),
            pltpu.SemaphoreType.DMA,
        ],
        compiler_params=pltpu.CompilerParams(
            collective_id=0, has_side_effects=True, vmem_limit_bytes=40 * 2**20
        ),
        name="exchange",
    )(sent)


def local(traces, valid, pair_list):
    owners = lax.axis_size("pairs")
    window_devs = lax.axis_size("win")
    me = lax.axis_index("pairs")
    samples = traces.shape[-1]
    per_window = traces.shape[2]
    windows = per_window * window_devs
    blk_count = traces.shape[0] // SB
    pair_count = pair_list.shape[0] // owners
    pairs = pair_count // window_devs
    capacity = max(1, 4 * pair_count // owners)
    series = ROWS * per_window
    masked = (traces * valid[:, None, :, None].astype(traces.dtype)).reshape(-1, samples)

    requests = pair_list.reshape(owners, 2 * pair_count)
    sources = requests // blk_count
    ids = jnp.arange(2 * pair_count, dtype=jnp.int32)
    earlier = ids[None, :] < ids[:, None]
    ranks = jnp.sum((sources[:, :, None] == sources[:, None, :]) & earlier[None], axis=-1)
    slots = jnp.arange(capacity, dtype=jnp.int32)
    found = (sources == me)[:, None, :] & (ranks[:, None, :] == slots[None, :, None])
    picked = jnp.sum(jnp.where(found, requests[:, None, :] % blk_count + 1, 0), axis=-1) - 1
    picked = jnp.broadcast_to(picked[:, None], (owners, window_devs, capacity)).reshape(-1, 1)
    serial = jnp.arange(series, dtype=jnp.int32)
    from_rows = jnp.where(picked < 0, -1, picked * series + serial).reshape(-1, 1)
    sending = from_rows == jnp.arange(masked.shape[0], dtype=jnp.int32)[None, :]
    sent = jnp.dot(sending.astype(jnp.bfloat16), masked, preferred_element_type=jnp.bfloat16)
    received = exchange(
        sent.reshape(owners * window_devs, capacity * series, samples), window_devs
    ).reshape(-1, samples)

    def kept(array):
        own = lax.dynamic_index_in_dim(array, me, 0, keepdims=False).reshape(pair_count, 2)
        own = lax.dynamic_slice_in_dim(own, lax.axis_index("win") * pairs, pairs, 0)
        return own.T[:, None, None, None, :]

    i = jnp.arange(ROWS, dtype=jnp.int32)[None, :, None, None, None]
    v = jnp.arange(window_devs, dtype=jnp.int32)[None, None, :, None, None]
    w = jnp.arange(per_window, dtype=jnp.int32)[None, None, None, :, None]
    slot = (kept(sources) * window_devs + v) * capacity + kept(ranks)
    wanted = (slot * ROWS + i) * per_window + w
    chosen = wanted.reshape(-1, 1) == jnp.arange(received.shape[0], dtype=jnp.int32)[None, :]
    x = jnp.dot(chosen.astype(jnp.bfloat16), received, preferred_element_type=jnp.bfloat16)
    return stack(x, pairs, windows)


def solution(mesh):
    in_specs = (
        P(("groups", "pairs"), None, "win", None),
        P(("groups", "pairs"), "win"),
        P("groups", None),
    )
    out_specs = P(("groups", "pairs", "win"), None, None)
    return jax.shard_map(local, mesh=mesh, in_specs=in_specs, out_specs=out_specs, check_vma=False)
```

```python
import functools
import math

import jax
import jax.numpy as jnp
import ml_dtypes
import numpy as np
from jax import lax
from jax.experimental import pallas as pl
from jax.experimental.pallas import tpu as pltpu
from jax.sharding import PartitionSpec as P

BAND = 64
SB = 2
ROWS = SB * 3
CORRS = ROWS * ROWS
TILE = 256


def tables(samples):
    period = 2 * samples
    angle = np.arange(period, dtype=np.float32) * np.float32(2.0 * math.pi / period)
    cosine, sine = np.cos(angle), np.sin(angle)
    index = np.arange(samples, dtype=np.int32)
    forward = index[:, None] * index[None, :] % period
    inverse = index[:, None] * (index[None, :] - samples // 2) % period
    weight = np.where(index[:, None] == 0, 1.0, 2.0).astype(np.float32) / np.float32(math.sqrt(period))
    first = np.stack([cosine[forward], -sine[forward]]).astype(ml_dtypes.bfloat16)
    second = np.stack([weight * cosine[inverse], -weight * sine[inverse]]).astype(ml_dtypes.bfloat16)
    return first, second


def stack_kernel(pairs, windows, x_ref, fwd_ref, band_ref, inv_ref, out_ref, white, cross):
    @pl.when(pl.program_id(0) == 0)
    def _():
        out_ref[...] = jnp.zeros_like(out_ref)

    x = x_ref[...]
    real = jnp.dot(x, fwd_ref[0], preferred_element_type=jnp.float32)
    imag = jnp.dot(x, fwd_ref[1], preferred_element_type=jnp.float32)
    magnitude = jnp.sqrt(real * real + imag * imag)
    high = magnitude.astype(jnp.bfloat16)
    low = (magnitude - high.astype(jnp.float32)).astype(jnp.bfloat16)
    band = jnp.dot(high, band_ref[...], preferred_element_type=jnp.float32) + jnp.dot(
        low, band_ref[...], preferred_element_type=jnp.float32
    )
    scale = 1.0 / (band + 1e-06)
    white[0] = (real * scale).astype(jnp.bfloat16).astype(jnp.float32)
    white[1] = (imag * scale).astype(jnp.bfloat16).astype(jnp.float32)
    for lane in range(0, TILE, 128):
        lanes = slice(lane, lane + 128)
        for p0 in range(0, pairs, 8):

            def value(side, i, w, part):
                row = ((side * ROWS + i) * windows + w) * pairs + p0
                return white[part, row : row + 8, lanes]

            for i in range(ROWS):
                mine = [(value(0, i, w, 0), value(0, i, w, 1)) for w in range(windows)]
                for j in range(ROWS):
                    re = im = None
                    for w in range(windows):
                        ar, ai = mine[w]
                        br, bi = value(1, j, w, 0), value(1, j, w, 1)
                        re_w = ar * br + ai * bi
                        im_w = ar * bi - ai * br
                        re = re_w if re is None else re + re_w
                        im = im_w if im is None else im + im_w
                    row = (i * ROWS + j) * pairs + p0
                    cross[row : row + 8, lanes] = re * (1.0 / windows)
                    cross[row : row + 8, TILE + lane : TILE + lane + 128] = im * (1.0 / windows)
    both = cross[...].astype(jnp.bfloat16)
    samples = out_ref.shape[-1]
    wide = 512
    for t in range(0, samples, wide):
        table = jnp.concatenate([inv_ref[0, :, t : t + wide], inv_ref[1, :, t : t + wide]], axis=0)
        out_ref[:, t : t + wide] += jnp.dot(both, table, preferred_element_type=jnp.float32)


def stack(x, pairs, windows):
    samples = x.shape[-1]
    first, second = tables(samples)
    runs = np.arange(TILE) // BAND
    band = ((runs[:, None] == runs[None, :]) / BAND).astype(ml_dtypes.bfloat16)
    out = pl.pallas_call(
        functools.partial(stack_kernel, pairs, windows),
        out_shape=jax.ShapeDtypeStruct((CORRS * pairs, samples), jnp.float32),
        grid=(samples // TILE,),
        in_specs=[
            pl.BlockSpec(x.shape, lambda j: (0, 0)),
            pl.BlockSpec((2, samples, TILE), lambda j: (0, 0, j)),
            pl.BlockSpec((TILE, TILE), lambda j: (0, 0)),
            pl.BlockSpec((2, TILE, samples), lambda j: (0, j, 0)),
        ],
        out_specs=pl.BlockSpec((CORRS * pairs, samples), lambda j: (0, 0)),
        scratch_shapes=[
            pltpu.VMEM((2, x.shape[0], TILE), jnp.float32),
            pltpu.VMEM((CORRS * pairs, 2 * TILE), jnp.float32),
        ],
        compiler_params=pltpu.CompilerParams(vmem_limit_bytes=56 * 2**20),
        cost_estimate=pl.CostEstimate(
            flops=4 * (x.shape[0] + pairs * CORRS) * samples * samples,
            bytes_accessed=8 * samples * samples + 4 * pairs * CORRS * samples,
            transcendentals=x.shape[0] * samples,
        ),
        name="stack",
    )(x, jnp.asarray(first), jnp.asarray(band), jnp.asarray(second))
    return out.reshape(CORRS, pairs, samples).transpose(1, 0, 2)


def gather_kernel(shape, own_ref, got_ref, send_sem, recv_sem, own_sem):
    long, wide, window_devs = shape
    cores = 2
    group = lax.axis_index("groups")
    me = lax.axis_index("pairs") * window_devs + lax.axis_index("win")
    z, y, c = me // (wide * cores), me // cores % wide, me % cores

    def slot_of(z_, y_, c_):
        return (z_ * wide + y_) * cores + c_

    ways = (
        slot_of(z + 1, y, c),
        slot_of(z - 1, y, c),
        slot_of(z, wide - 1 - y, c),
        slot_of(z, y, cores - 1 - c),
    )
    RIGHT, LEFT, ACROSS, CORE = range(4)

    def device(index):
        return (group, index // window_devs, index % window_devs)

    def copy(way, slot, src=None):
        return pltpu.make_async_remote_copy(
            src_ref=got_ref.at[slot] if src is None else src,
            dst_ref=got_ref.at[slot],
            send_sem=send_sem.at[way, slot],
            recv_sem=recv_sem.at[slot],
            device_id=device(ways[way]),
            device_id_type=pl.DeviceIdType.MESH,
        )

    def greet(way):
        pl.semaphore_signal(
            barrier, inc=1, device_id=device(ways[way]), device_id_type=pl.DeviceIdType.MESH
        )

    has_right, has_left = z < long - 1, z > 0
    barrier = pltpu.get_barrier_semaphore()
    pl.when(has_right)(lambda: greet(RIGHT))
    pl.when(has_left)(lambda: greet(LEFT))
    if wide > 1:
        greet(ACROSS)
    greet(CORE)
    ends = jnp.where(has_right, 1, 0) + jnp.where(has_left, 1, 0)
    pl.semaphore_wait(barrier, ends + (2 if wide > 1 else 1))

    pl.when(has_right)(lambda: copy(RIGHT, me, own_ref).start())
    pl.when(has_left)(lambda: copy(LEFT, me, own_ref).start())
    if wide > 1:
        copy(ACROSS, me, own_ref).start()
    copy(CORE, me, own_ref).start()
    own = pltpu.make_async_copy(own_ref, got_ref.at[me], own_sem)
    own.start()

    def pass_on(slot, way, more):
        copy(CORE, slot, own_ref).wait_recv()
        pl.when(more)(lambda: copy(way, slot).start())
        if wide > 1:
            copy(ACROSS, slot).start()
        copy(CORE, slot).start()

    @pl.loop(0, long - 1)
    def _(s):
        pl.when(s < z)(lambda: pass_on(slot_of(z - 1 - s, y, c), RIGHT, has_right))
        pl.when(z + 1 + s < long)(lambda: pass_on(slot_of(z + 1 + s, y, c), LEFT, has_left))

    if wide > 1:

        def pass_across(z_):
            slot = slot_of(z_, wide - 1 - y, c)
            copy(CORE, slot, own_ref).wait_recv()
            copy(CORE, slot).start()

        pass_across(z)

        @pl.loop(0, long - 1)
        def _(s):
            pl.when(s < z)(lambda: pass_across(z - 1 - s))
            pl.when(z + 1 + s < long)(lambda: pass_across(z + 1 + s))

    own.wait()

    @pl.loop(0, long)
    def _(z_):
        for y_ in range(wide):
            copy(CORE, slot_of(z_, y_, cores - 1 - c), own_ref).wait_recv()
            copy(CORE, slot_of(z_, y_, c)).wait_send()
        slot = slot_of(z_, y, c)
        if wide > 1:
            copy(ACROSS, slot).wait_send()
        pl.when(has_right & (z_ <= z))(lambda: copy(RIGHT, slot).wait_send())
        pl.when(has_left & (z_ >= z))(lambda: copy(LEFT, slot).wait_send())


def gather(own, owners, window_devs):
    count = owners * window_devs
    wide = 2 if window_devs == 1 else 1
    shape = (count // (2 * wide), wide, window_devs)
    return pl.pallas_call(
        functools.partial(gather_kernel, shape),
        out_shape=jax.ShapeDtypeStruct((count,) + own.shape, own.dtype),
        in_specs=[pl.BlockSpec(memory_space=pltpu.VMEM)],
        out_specs=pl.BlockSpec(memory_space=pltpu.VMEM),
        scratch_shapes=[
            pltpu.SemaphoreType.DMA((4, count)),
            pltpu.SemaphoreType.DMA((count,)),
            pltpu.SemaphoreType.DMA,
        ],
        compiler_params=pltpu.CompilerParams(
            collective_id=0, has_side_effects=True, vmem_limit_bytes=40 * 2**20
        ),
        name="gather",
    )(own)


def local(traces, valid, pair_list):
    owners = lax.axis_size("pairs")
    window_devs = lax.axis_size("win")
    samples = traces.shape[-1]
    per_window = traces.shape[2]
    windows = per_window * window_devs
    blk_count = traces.shape[0] // SB
    pairs = pair_list.shape[0] // (owners * window_devs)
    own_rows = blk_count * ROWS * per_window
    masked = traces * valid[:, None, :, None].astype(traces.dtype)
    everything = gather(masked.reshape(own_rows, samples), owners, window_devs)
    everything = everything.reshape(-1, samples)
    place = lax.axis_index("pairs") * window_devs + lax.axis_index("win")
    mine = lax.dynamic_slice_in_dim(pair_list, place * pairs, pairs, 0).T
    blocks = mine[:, None, None, None, :]
    i = jnp.arange(ROWS)[None, :, None, None, None]
    v = jnp.arange(window_devs)[None, None, :, None, None]
    w = jnp.arange(per_window)[None, None, None, :, None]
    device = blocks // blk_count * window_devs + v
    wanted = device * own_rows + ((blocks % blk_count) * ROWS + i) * per_window + w
    chosen = wanted.reshape(-1, 1) == jnp.arange(everything.shape[0])[None, :]
    x = jnp.dot(chosen.astype(jnp.bfloat16), everything, preferred_element_type=jnp.bfloat16)
    return stack(x, pairs, windows)


def solution(mesh):
    in_specs = (
        P(("groups", "pairs"), None, "win", None),
        P(("groups", "pairs"), "win"),
        P("groups", None),
    )
    out_specs = P(("groups", "pairs", "win"), None, None)
    return jax.shard_map(local, mesh=mesh, in_specs=in_specs, out_specs=out_specs, check_vma=False)
```
